32 devices in a mesh: dp: 16 (over z, x, core), tensor: 2 (over y).
Axes of the slice: x: 2, y: 2, z: 4, core: 2. Of those that a mesh axis runs over, the one named last changes fastest.
Arguments:
- tokens: bfloat16 [32768, 1024], P(('dp', 'tensor')), may hold values from -6 to 6
- first_gain: float32 [1024], replicated, may hold values from 0.1 to 1.9
- first_bias: float32 [1024], replicated, may hold values from -3 to 3
- qkv_weight: bfloat16 [1024, 3, 1024], P(None, None, 'tensor'), may hold values from -0.1875 to 0.1875
- qv_bias: float32 [2, 1024], P(None, 'tensor'), may hold values from -3 to 3
- out_weight: bfloat16 [1024, 1024], P('tensor'), may hold values from -1.5 to 1.5
- out_bias: float32 [1024], replicated, may hold values from -3 to 3
- attention_scale: float32 [1024], replicated, may hold values from 0.5 to 2
- second_gain: float32 [1024], replicated, may hold values from 0.1 to 1.9
- second_bias: float32 [1024], replicated, may hold values from -3 to 3
- up_weight: bfloat16 [1024, 4096], P(None, 'tensor'), may hold values from -0.1875 to 0.1875
- up_bias: float32 [4096], P('tensor'), may hold values from -3 to 3
- down_weight: bfloat16 [4096, 1024], P('tensor'), may hold values from -0.09375 to 0.09375
- down_bias: float32 [1024], replicated, may hold values from -3 to 3
- mlp_scale: float32 [1024], replicated, may hold values from 0.5 to 2
- cotangent: bfloat16 [32768, 1024], P(('dp', 'tensor')), may hold values from -6 to 6
Outputs:
- block_out: bfloat16 [32768, 1024], P(('dp', 'tensor'))
- input_grad: float32 [32768, 1024], P(('dp', 'tensor'))
- first_gain_grad: float32 [1024], replicated
- first_bias_grad: float32 [1024], replicated
- qkv_weight_grad: float32 [1024, 3, 1024], P(None, None, 'tensor')
- qv_bias_grad: float32 [2, 1024], P(None, 'tensor')
- out_weight_grad: float32 [1024, 1024], P('tensor')
- out_bias_grad: float32 [1024], replicated
- attention_scale_grad: float32 [1024], replicated
- second_gain_grad: float32 [1024], replicated
- second_bias_grad: float32 [1024], replicated
- up_weight_grad: float32 [1024, 4096], P(None, 'tensor')
- up_bias_grad: float32 [4096], P('tensor')
- down_weight_grad: float32 [4096, 1024], P('tensor')
- down_bias_grad: float32 [1024], replicated
- mlp_scale_grad: float32 [1024], replicated
The draws below stay inside these ranges and needn't reach their ends.
All inputs are finite; a program needn't handle non-finite values.
Results may differ from the reference program's by a relative error of at most 0.019.
Values may be sent and summed in bfloat16 or wider, within the bound.
A program may use at most 256 MiB of HBM per device.

```python
import math
import jax
import jax.numpy as jnp
from jax import lax

D = 1024
HEADS = 16
HD = 64
FF = 4096
SEQ = 1024
IMG_DEV = 2
TOKENS = 32768
N_DP = 16


def level_of(stream_key, dims, cuts, low, top_value):
    factor_of, own = 1.0, jax.random.fold_in(stream_key, 6)
    for dim, blocks in cuts:
        steps = jnp.exp(jax.random.uniform(jax.random.fold_in(own, dim), (blocks,), jnp.float32, low / len(cuts), top_value / len(cuts)))
        factor_of = factor_of * jnp.repeat(steps, dims[dim] // blocks).reshape([-1 if axis == dim else 1 for axis in range(len(dims))])
    return factor_of


def centred(key, shape, scale, limit, cuts=(), dtype=jnp.bfloat16):
    array = jax.random.normal(key, shape, jnp.float32) * scale
    if len(cuts) > 0:
        array = level_of(key, shape, cuts, -0.22, 0.18) * array
    return jnp.clip(array, min=-limit, max=limit).astype(dtype)


def setup_inputs(seed: int = 0) -> dict:
    seeds = jax.random.split(jax.random.key(seed), 17)
    return {
        "tokens": centred(seeds[0], (TOKENS, D), 1.0, 6.0, ((0, 32),)),
        "first_gain": jnp.clip(1.0 + 0.18 * jax.random.normal(seeds[1], (D,), jnp.float32), 0.1, 1.9),
        "first_bias": centred(seeds[2], (D,), 0.5, 3.0, (), jnp.float32),
        "qkv_weight": centred(seeds[3], (D, 3, D), D ** -0.5, 0.1875, ((2, 2),)),
        "qv_bias": centred(seeds[4], (2, D), 0.5, 3.0, ((1, 2),), jnp.float32),
        "out_weight": centred(seeds[5], (D, D), (max(1, D // 64)) ** -0.5, 1.5, ((0, 2),)),
        "out_bias": centred(seeds[6], (D,), 0.5, 3.0, (), jnp.float32),
        "attention_scale": jnp.clip(jnp.exp(jax.random.uniform(seeds[7], (D,), jnp.float32, math.log(0.5), math.log(2.0))), 0.5, 2.0),
        "second_gain": jnp.clip(1.0 + 0.18 * jax.random.normal(seeds[8], (D,), jnp.float32), 0.1, 1.9),
        "second_bias": centred(seeds[9], (D,), 0.5, 3.0, (), jnp.float32),
        "up_weight": centred(seeds[10], (D, FF), D ** -0.5, 0.1875, ((1, 2),)),
        "up_bias": centred(seeds[11], (FF,), 0.5, 3.0, ((0, 2),), jnp.float32),
        "down_weight": centred(seeds[12], (FF, D), FF ** -0.5, 0.09375, ((0, 2),)),
        "down_bias": centred(seeds[13], (D,), 0.5, 3.0, (), jnp.float32),
        "mlp_scale": jnp.clip(jnp.exp(jax.random.uniform(seeds[14], (D,), jnp.float32, math.log(0.5), math.log(2.0))), 0.5, 2.0),
        "cotangent": centred(seeds[15], (TOKENS, D), 1.0, 6.0, ((0, 32),)),
    }


EPSILON = 1e-06
HIGH = lax.Precision.HIGHEST

@jax.custom_vjp
def low(v):
    return lax.optimization_barrier(v.astype(jnp.bfloat16)).astype(jnp.float32)

@jax.custom_vjp
def low_back(v):
    return v

def low_keep(v):
    return (low(v), None)

def low_pass(kept, grad):
    return (grad,)

def back_keep(v):
    return (v, None)

def back_low(kept, grad):
    return (low(grad),)
low.defvjp(low_keep, low_pass)
low_back.defvjp(back_keep, back_low)

def norm_rows(values, gain, shift):
    center = values - lax.optimization_barrier(jnp.mean(values, axis=-1, keepdims=True))
    spread = lax.optimization_barrier(jnp.mean(center * center, axis=-1, keepdims=True))
    return center * lax.rsqrt(spread + EPSILON) * gain + shift

def matmul(left, right):
    return jnp.dot(left, right, precision=HIGH, preferred_element_type=jnp.float32)

def exact_gelu(values):
    return jax.nn.gelu(values, approximate=False)

def attend_block(query, keys, values):
    scores = low_back(jnp.einsum('qhd,khd->hqk', query, keys, precision=HIGH) * HD ** (-0.5))
    row_peak = lax.optimization_barrier(jnp.max(scores, axis=-1, keepdims=True))
    powers = jnp.exp(scores - row_peak)
    probs = low(powers / lax.optimization_barrier(jnp.sum(powers, axis=-1, keepdims=True)))
    return jnp.einsum('hqk,khd->qhd', probs, values, precision=HIGH)

def attend_image(parts):
    image_query, image_keys, image_values = parts
    block = min(512, SEQ)
    blocks = image_query.reshape(SEQ // block, block, HEADS, HD)
    mixed = lax.map(jax.checkpoint(lambda piece: attend_block(piece, image_keys, image_values)), blocks)
    return mixed.reshape(SEQ, HEADS, HD)

def forward(inputs, params):
    g_one, b_one, qkv_w, qv_b, out_w, out_b, scale_one, g_two, b_two, up_w, up_b, down_w, down_b, scale_two = params
    normed = low(norm_rows(inputs, g_one, b_one))
    query = low(low_back(matmul(normed, qkv_w[:, 0, :]) + qv_b[0]))
    keys = low(low_back(matmul(normed, qkv_w[:, 1, :])))
    values = low(low_back(matmul(normed, qkv_w[:, 2, :]) + qv_b[1]))
    images = inputs.shape[0] // SEQ
    shaped = (images, SEQ, HEADS, HD)
    mixed = lax.map(attend_image, (query.reshape(shaped), keys.reshape(shaped), values.reshape(shaped)))
    mixed = low(low_back(mixed.reshape(inputs.shape[0], D)))
    attention = low_back(matmul(mixed, out_w) + out_b)
    after_attention = inputs + scale_one * attention
    second = low(norm_rows(after_attention, g_two, b_two))
    pre_act = low_back(matmul(second, up_w) + up_b)
    hidden = low(exact_gelu(pre_act))
    feed = low_back(matmul(hidden, down_w) + down_b)
    return after_attention + scale_two * feed

def reference(tokens, first_gain, first_bias, qkv_weight, qv_bias, out_weight, out_bias, attention_scale, second_gain, second_bias, up_weight, up_bias, down_weight, down_bias, mlp_scale, cotangent):
    params = tuple((p.astype(jnp.float32) for p in (first_gain, first_bias, qkv_weight, qv_bias, out_weight, out_bias, attention_scale, second_gain, second_bias, up_weight, up_bias, down_weight, down_bias, mlp_scale)))
    group = IMG_DEV * SEQ
    inputs = tokens.astype(jnp.float32).reshape(N_DP, group, D)
    upstream = cotangent.astype(jnp.float32).reshape(N_DP, group, D)

    def step(totals, pair):
        part_in, part_up = pair
        result, pull = jax.vjp(forward, part_in, params)
        grad_in, grad_params = pull(part_up)
        totals = jax.tree.map(lambda first, second: first + second, totals, grad_params)
        return (totals, (result.astype(jnp.bfloat16), grad_in))
    zeros = jax.tree.map(jnp.zeros_like, params)
    totals, (results, grads) = lax.scan(step, zeros, (inputs, upstream))
    return (results.reshape(-1, D), grads.reshape(-1, D), totals[0], totals[1], totals[2], totals[3], totals[4], totals[5], totals[6], totals[7], totals[8], totals[9], totals[10], totals[11], totals[12], totals[13])
```

```python
import math

import jax
import jax.numpy as jnp
from jax import lax
from jax.experimental import pallas as pl
from jax.experimental.pallas import tpu as pltpu
from jax.sharding import PartitionSpec as P

HD = 64
SEQ = 1024


EPSILON = 1e-06


def norm_rows(values, gain, shift):
    center = values - jnp.mean(values, axis=-1, keepdims=True)
    spread = jnp.mean(center * center, axis=-1, keepdims=True)
    return center * lax.rsqrt(spread + EPSILON) * gain + shift


def exact_gelu(values):
    return jax.nn.gelu(values, approximate=False)


def attend_forward(query, keys, values):
    factor = query.shape[-1] ** (-0.5)
    scores = jnp.einsum("qhd,khd->hqk", query, keys, preferred_element_type=jnp.float32) * factor
    row_peak = jnp.max(scores, axis=-1, keepdims=True)
    powers = jnp.exp(scores - row_peak)
    totals = jnp.sum(powers, axis=-1, keepdims=True)
    probs = (powers / totals).astype(jnp.bfloat16)
    mixed = jnp.einsum("hqk,khd->qhd", probs, values, preferred_element_type=jnp.float32).astype(
        jnp.bfloat16
    )
    return (mixed, row_peak[..., 0] + jnp.log(totals[..., 0]))


def attend_backward(carry, piece, keys, values):
    query, grad_out, log_totals = piece
    factor = query.shape[-1] ** (-0.5)
    scores = jnp.einsum("qhd,khd->hqk", query, keys, preferred_element_type=jnp.float32) * factor
    probs = jnp.exp(scores - log_totals[..., None])
    low_probs = probs.astype(jnp.bfloat16)
    grad_values = carry[1] + jnp.einsum(
        "hqk,qhd->khd", low_probs, grad_out, preferred_element_type=jnp.float32
    )
    grad_probs = jnp.einsum("qhd,khd->hqk", grad_out, values, preferred_element_type=jnp.float32)
    delta = jnp.sum(grad_probs * probs, axis=-1, keepdims=True)
    grad_scores = (probs * (grad_probs - delta)).astype(jnp.bfloat16)
    grad_query = (
        jnp.einsum("hqk,khd->qhd", grad_scores, keys, preferred_element_type=jnp.float32) * factor
    ).astype(jnp.bfloat16)
    grad_keys = (
        carry[0]
        + jnp.einsum("hqk,qhd->khd", grad_scores, query, preferred_element_type=jnp.float32)
        * factor
    )
    return ((grad_keys, grad_values), grad_query)


def general_body(
    tokens,
    first_gain,
    first_bias,
    qkv_weight,
    qv_bias,
    out_weight,
    out_bias,
    attention_scale,
    second_gain,
    second_bias,
    up_weight,
    up_bias,
    down_weight,
    down_bias,
    mlp_scale,
    cotangent,
):
    local_rows, width = tokens.shape
    group_size = lax.axis_size("tensor")
    total_rows = local_rows * group_size
    columns = qkv_weight.shape[2]
    heads_here = columns // HD
    block = min(512, SEQ)
    block_count = SEQ // block
    images = total_rows // SEQ
    image_shape = (images, SEQ, heads_here, HD)
    qkv_flat = qkv_weight.reshape(width, 3 * columns)
    residual = tokens.astype(jnp.float32)
    first_norm = norm_rows(residual, first_gain, first_bias).astype(jnp.bfloat16)
    normed = lax.all_gather(first_norm, "tensor", axis=0, tiled=True)
    projected = jnp.dot(normed, qkv_flat, preferred_element_type=jnp.float32)
    query = (projected[:, :columns] + qv_bias[0]).astype(jnp.bfloat16)
    keys = projected[:, columns : 2 * columns].astype(jnp.bfloat16)
    values = (projected[:, 2 * columns :] + qv_bias[1]).astype(jnp.bfloat16)

    def forward_image(parts):
        image_query, image_keys, image_values = parts
        blocks = image_query.reshape(block_count, block, heads_here, HD)
        mixed_blocks, log_blocks = lax.map(
            lambda piece: attend_forward(piece, image_keys, image_values), blocks
        )
        return (mixed_blocks.reshape(SEQ, heads_here, HD), log_blocks)

    mixed, log_totals = lax.map(
        forward_image,
        (query.reshape(image_shape), keys.reshape(image_shape), values.reshape(image_shape)),
    )
    mixed = mixed.reshape(total_rows, columns)
    attention = (
        lax.psum_scatter(
            jnp.dot(mixed, out_weight, preferred_element_type=jnp.float32),
            "tensor",
            scatter_dimension=0,
            tiled=True,
        )
        + out_bias
    )
    after_attention = residual + attention_scale * attention
    second_norm = norm_rows(after_attention, second_gain, second_bias).astype(jnp.bfloat16)
    normed_second = lax.all_gather(second_norm, "tensor", axis=0, tiled=True)
    pre_act = jnp.dot(normed_second, up_weight, preferred_element_type=jnp.float32) + up_bias
    activated, gelu_pull = jax.vjp(exact_gelu, pre_act)
    hidden = activated.astype(jnp.bfloat16)
    feed = (
        lax.psum_scatter(
            jnp.dot(hidden, down_weight, preferred_element_type=jnp.float32).astype(jnp.bfloat16),
            "tensor",
            scatter_dimension=0,
            tiled=True,
        ).astype(jnp.float32)
        + down_bias
    )
    block_out = (after_attention + mlp_scale * feed).astype(jnp.bfloat16)
    upstream = cotangent.astype(jnp.float32)
    grad_mlp_scale = jnp.sum(upstream * feed, axis=0)
    grad_feed = (upstream * mlp_scale).astype(jnp.bfloat16)
    grad_down_bias = jnp.sum(grad_feed.astype(jnp.float32), axis=0)
    feed_rows = lax.all_gather(grad_feed, "tensor", axis=0, tiled=True)
    grad_down_weight = jnp.dot(hidden.T, feed_rows, preferred_element_type=jnp.float32)
    grad_hidden = jnp.dot(feed_rows, down_weight.T, preferred_element_type=jnp.float32)
    grad_pre = gelu_pull(grad_hidden)[0].astype(jnp.bfloat16)
    grad_up_bias = jnp.sum(grad_pre.astype(jnp.float32), axis=0)
    grad_up_weight = jnp.dot(normed_second.T, grad_pre, preferred_element_type=jnp.float32)
    grad_second = lax.psum_scatter(
        jnp.dot(grad_pre, up_weight.T, preferred_element_type=jnp.float32),
        "tensor",
        scatter_dimension=0,
        tiled=True,
    )
    second_value, second_pull = jax.vjp(norm_rows, after_attention, second_gain, second_bias)
    grad_after, grad_second_gain, grad_second_bias = second_pull(grad_second)
    grad_after = grad_after + upstream
    grad_attention_scale = jnp.sum(grad_after * attention, axis=0)
    grad_attention = (grad_after * attention_scale).astype(jnp.bfloat16)
    grad_out_bias = jnp.sum(grad_attention.astype(jnp.float32), axis=0)
    attention_rows = lax.all_gather(grad_attention, "tensor", axis=0, tiled=True)
    grad_out_weight = jnp.dot(mixed.T, attention_rows, preferred_element_type=jnp.float32)
    grad_mixed = jnp.dot(attention_rows, out_weight.T, preferred_element_type=jnp.float32).astype(
        jnp.bfloat16
    )

    def backward_image(parts):
        image_query, image_keys, image_values, image_grad, image_logs = parts
        blocks = (
            image_query.reshape(block_count, block, heads_here, HD),
            image_grad.reshape(block_count, block, heads_here, HD),
            image_logs,
        )
        zeros = jnp.zeros((SEQ, heads_here, HD), jnp.float32)
        sums, grad_query_blocks = lax.scan(
            lambda carry, piece: attend_backward(carry, piece, image_keys, image_values),
            (zeros, zeros),
            blocks,
        )
        return (
            grad_query_blocks.reshape(SEQ, heads_here, HD),
            sums[0].astype(jnp.bfloat16),
            sums[1].astype(jnp.bfloat16),
        )

    grad_query, grad_keys, grad_values = lax.map(
        backward_image,
        (
            query.reshape(image_shape),
            keys.reshape(image_shape),
            values.reshape(image_shape),
            grad_mixed.reshape(image_shape),
            log_totals,
        ),
    )
    grad_query = grad_query.reshape(total_rows, columns)
    grad_keys = grad_keys.reshape(total_rows, columns)
    grad_values = grad_values.reshape(total_rows, columns)
    grad_qv_bias = jnp.stack(
        [
            jnp.sum(grad_query.astype(jnp.float32), axis=0),
            jnp.sum(grad_values.astype(jnp.float32), axis=0),
        ]
    )
    grad_projected = jnp.concatenate([grad_query, grad_keys, grad_values], axis=1)
    grad_qkv_weight = jnp.dot(normed.T, grad_projected, preferred_element_type=jnp.float32).reshape(
        width, 3, columns
    )
    grad_first = lax.psum_scatter(
        jnp.dot(grad_projected, qkv_flat.T, preferred_element_type=jnp.float32).astype(
            jnp.bfloat16
        ),
        "tensor",
        scatter_dimension=0,
        tiled=True,
    ).astype(jnp.float32)
    first_value, first_pull = jax.vjp(norm_rows, residual, first_gain, first_bias)
    grad_input, grad_first_gain, grad_first_bias = first_pull(grad_first)
    grad_input = grad_input + grad_after
    weights = (
        lax.psum(grad_qkv_weight.astype(jnp.bfloat16), "dp").astype(jnp.float32),
        lax.psum(grad_qv_bias.astype(jnp.bfloat16), "dp").astype(jnp.float32),
        lax.psum(grad_out_weight.astype(jnp.bfloat16), "dp").astype(jnp.float32),
        lax.psum(grad_up_weight.astype(jnp.bfloat16), "dp").astype(jnp.float32),
        lax.psum(grad_up_bias.astype(jnp.bfloat16), "dp").astype(jnp.float32),
        lax.psum(grad_down_weight.astype(jnp.bfloat16), "dp").astype(jnp.float32),
    )
    shared = lax.psum(
        (
            grad_first_gain,
            grad_first_bias,
            grad_out_bias,
            grad_attention_scale,
            grad_second_gain,
            grad_second_bias,
            grad_down_bias,
            grad_mlp_scale,
        ),
        ("dp", "tensor"),
    )
    return (
        block_out,
        grad_input,
        shared[0],
        shared[1],
        weights[0],
        weights[1],
        weights[2],
        shared[2],
        shared[3],
        shared[4],
        shared[5],
        weights[3],
        weights[4],
        weights[5],
        shared[6],
        shared[7],
    )


CHUNK = 256
PAIR = 2 * HD


def contract(left, right):
    return jnp.dot(left, right, preferred_element_type=jnp.float32)


def contract_last(left, right):
    return lax.dot_general(left, right, (((1,), (1,)), ((), ())), preferred_element_type=jnp.float32)


def contract_first(left, right):
    return lax.dot_general(left, right, (((0,), (0,)), ((), ())), preferred_element_type=jnp.float32)


def turned(values):
    return values.astype(jnp.float32).T.astype(jnp.bfloat16)


def pair_forward(query_ref, keys_ref, values_ref, mixed_ref, logs_ref):
    keys = keys_ref[...]
    query_t = turned(query_ref[...] * jnp.bfloat16(HD**-0.5))
    values_t = turned(values_ref[...])
    row_head = lax.broadcasted_iota(jnp.int32, (PAIR, SEQ), 0) // HD
    for head in range(2):
        own_query = jnp.where(row_head == head, query_t, jnp.zeros_like(query_t))
        own_values = values_t[head * HD : (head + 1) * HD]
        parts = []
        for start in range(0, SEQ, CHUNK):
            scores = contract(keys, own_query[:, start : start + CHUNK])
            peak = jnp.max(scores, axis=0, keepdims=True)
            powers = jnp.exp(scores - peak)
            totals = jnp.sum(powers, axis=0, keepdims=True)
            parts.append(contract(own_values, powers.astype(jnp.bfloat16)) / totals)
            logs_ref[0, head : head + 1, start : start + CHUNK] = peak + jnp.log(totals)
        mixed_ref[:, head * HD : (head + 1) * HD] = jnp.concatenate(parts, axis=1).T.astype(jnp.bfloat16)


def pair_backward(
    query_ref, keys_ref, values_ref, grad_ref, logs_ref, dq_ref, dk_ref, dv_ref, dk_sum, dv_sum
):
    keys = keys_ref[...]
    values = values_ref[...]
    grad = grad_ref[...]
    query = query_ref[...] * jnp.bfloat16(HD**-0.5)
    query_t = turned(query)
    grad_t = turned(grad)
    keys_t = turned(keys)
    row_head = lax.broadcasted_iota(jnp.int32, (PAIR, SEQ), 0) // HD
    lane_head = lax.broadcasted_iota(jnp.int32, (SEQ, PAIR), 1) // HD
    zero = jnp.zeros_like(query)
    zero_t = jnp.zeros_like(query_t)
    for head in range(2):
        own_query_t = jnp.where(row_head == head, query_t, zero_t)
        own_grad_t = jnp.where(row_head == head, grad_t, zero_t)
        own_query = jnp.where(lane_head == head, query, zero)
        own_grad = jnp.where(lane_head == head, grad, zero)
        own_keys_t = keys_t[head * HD : (head + 1) * HD]
        parts = []
        for start in range(0, SEQ, CHUNK):
            cut = slice(start, start + CHUNK)
            scores = contract(keys, own_query_t[:, cut])
            probs = jnp.exp(scores - logs_ref[0, head : head + 1, cut])
            grad_probs = contract(values, own_grad_t[:, cut])
            delta = jnp.sum(grad_probs * probs, axis=0, keepdims=True)
            grad_scores = (probs * (grad_probs - delta)).astype(jnp.bfloat16)
            dv_part = contract(probs.astype(jnp.bfloat16), own_grad[cut])
            dk_part = contract(grad_scores, own_query[cut])
            if head == 0 and start == 0:
                dv_sum[...] = dv_part
                dk_sum[...] = dk_part
            else:
                dv_sum[...] += dv_part
                dk_sum[...] += dk_part
            parts.append(contract(own_keys_t, grad_scores) * HD**-0.5)
        dq_ref[:, head * HD : (head + 1) * HD] = jnp.concatenate(parts, axis=1).T.astype(jnp.bfloat16)
    dk_ref[...] = dk_sum[...].astype(jnp.bfloat16)
    dv_ref[...] = dv_sum[...].astype(jnp.bfloat16)


def part_spec(offset):
    return pl.BlockSpec((SEQ, PAIR), lambda image, pair: (image, offset + pair))


def logs_spec(pairs):
    return pl.BlockSpec((1, 2, SEQ), lambda image, pair: (image * pairs + pair, 0, 0))


def attend(projected):
    rows, columns = projected.shape[0], projected.shape[1] // 3
    pairs, images = columns // PAIR, rows // SEQ
    area = images * columns // HD * SEQ * SEQ
    return pl.pallas_call(
        pair_forward,
        grid=(images, pairs),
        in_specs=[part_spec(0), part_spec(pairs), part_spec(2 * pairs)],
        out_specs=[part_spec(0), logs_spec(pairs)],
        out_shape=[
            jax.ShapeDtypeStruct((rows, columns), jnp.bfloat16),
            jax.ShapeDtypeStruct((images * pairs, 2, SEQ), jnp.float32),
        ],
        compiler_params=pltpu.CompilerParams(vmem_limit_bytes=48 * 2**20),
        cost_estimate=pl.CostEstimate(
            flops=16 * area * HD, bytes_accessed=8 * rows * columns, transcendentals=area
        ),
    )(projected, projected, projected)


def attend_grad(projected, grad_mixed, logs):
    rows, columns = grad_mixed.shape
    pairs, images = columns // PAIR, rows // SEQ
    area = images * columns // HD * SEQ * SEQ
    return pl.pallas_call(
        pair_backward,
        grid=(images, pairs),
        in_specs=[
            part_spec(0),
            part_spec(pairs),
            part_spec(2 * pairs),
            part_spec(0),
            logs_spec(pairs),
        ],
        out_specs=[part_spec(0)] * 3,
        out_shape=[jax.ShapeDtypeStruct((rows, columns), jnp.bfloat16)] * 3,
        scratch_shapes=[pltpu.VMEM((SEQ, PAIR), jnp.float32)] * 2,
        compiler_params=pltpu.CompilerParams(vmem_limit_bytes=48 * 2**20),
        cost_estimate=pl.CostEstimate(
            flops=40 * area * HD, bytes_accessed=14 * rows * columns, transcendentals=area
        ),
    )(projected, projected, projected, grad_mixed, logs)


def over_group(values):
    return lax.ppermute(values, "tensor", [(0, 1), (1, 0)])


def over_pair(values):
    size = lax.axis_size("dp")
    return lax.ppermute(values, "dp", [(index, index ^ 1) for index in range(size)])


def fetch(weight, axis, parity):
    half = weight.shape[axis] // 2
    near = over_group(lax.dynamic_slice_in_dim(weight, parity * half, half, axis))
    return jnp.concatenate([near, over_pair(near)], axis=axis)


def sum_everywhere(own, other, axis, parity, after):
    half = own.shape[axis] // 2
    keep = lax.dynamic_slice_in_dim(own, parity * half, half, axis)
    give = lax.dynamic_slice_in_dim(own, (1 - parity) * half, half, axis)
    other_keep = lax.slice_in_dim(other, 0, half, axis=axis)
    other_give = lax.slice_in_dim(other, half, 2 * half, axis=axis)
    other_sum = other_keep + over_pair(other_give)
    own_sum = keep + over_pair(give)
    quarter = own_sum + over_group(other_sum)
    if after is not None:
        quarter, after = lax.optimization_barrier((quarter, after))
    size = lax.axis_size("dp")
    groups = [list(range(0, size, 2)), list(range(1, size, 2))]
    return lax.psum(quarter, "dp", axis_index_groups=groups), after


def both_halves(summed, axis, parity):
    partner = over_pair(summed)
    low = jnp.where(parity == 0, summed, partner)
    high = jnp.where(parity == 0, partner, summed)
    return jnp.concatenate([low, high], axis=axis).astype(jnp.float32)


def image_body(
    tokens,
    first_gain,
    first_bias,
    qkv_weight,
    qv_bias,
    out_weight,
    out_bias,
    attention_scale,
    second_gain,
    second_bias,
    up_weight,
    up_bias,
    down_weight,
    down_bias,
    mlp_scale,
    cotangent,
):
    width = tokens.shape[1]
    columns = qkv_weight.shape[2]
    units = up_weight.shape[1]
    parity = lax.axis_index("dp") % 2
    low = jnp.bfloat16

    def in_order(values):
        half = values.shape[-1] // 2
        turned_round = jnp.concatenate([values[..., half:], values[..., :half]], axis=-1)
        return jnp.where(parity == 0, values, turned_round)

    qkv_own = qkv_weight.reshape(width, 3 * columns)
    half = columns // 2
    sent = jnp.concatenate(
        [
            lax.dynamic_slice_in_dim(qkv_own, j * columns + parity * half, half, 1)
            for j in range(3)
        ],
        axis=1,
    )
    near = over_group(sent)
    far = over_pair(near)
    qkv_other = jnp.concatenate(
        [piece[:, j * half : (j + 1) * half] for j in range(3) for piece in (near, far)], axis=1
    )
    biases = over_group(jnp.concatenate([qv_bias.reshape(-1), up_bias]))
    qv_other = in_order(biases[: 2 * columns].reshape(2, columns))
    up_bias_other = in_order(biases[2 * columns :])
    out_other = fetch(out_weight, 0, parity)
    up_other = fetch(up_weight, 1, parity)
    down_other = fetch(down_weight, 0, parity)
    qkv_pair = (qkv_own, qkv_other)
    qv_pair = (qv_bias, qv_other)
    out_pair = (out_weight, out_other)
    up_pair = (up_weight, up_other)
    up_bias_pair = (up_bias, up_bias_other)
    down_pair = (down_weight, down_other)

    residual = tokens.astype(jnp.float32)
    first_norm = norm_rows(residual, first_gain, first_bias).astype(low)
    projected = []
    mixed = []
    logs = []
    for weight, bias in zip(qkv_pair, qv_pair):
        shift = jnp.concatenate([bias[0], jnp.zeros_like(bias[0]), bias[1]])
        projected.append((contract(first_norm, weight) + shift).astype(low))
        part, log_part = attend(projected[-1])
        mixed.append(part)
        logs.append(log_part)
    attention = contract(mixed[0], out_pair[0]) + contract(mixed[1], out_pair[1]) + out_bias
    after_attention = residual + attention_scale * attention
    second_norm = norm_rows(after_attention, second_gain, second_bias).astype(low)
    hidden = []
    slopes = []
    for weight, bias in zip(up_pair, up_bias_pair):
        pre_act = contract(second_norm, weight) + bias
        spread = 0.5 * (1.0 + lax.erf(pre_act * math.sqrt(0.5)))
        slope = spread + pre_act * jnp.exp(-0.5 * pre_act * pre_act) * (1.0 / math.sqrt(2.0 * math.pi))
        act, slope = lax.optimization_barrier(((pre_act * spread).astype(low), slope.astype(low)))
        hidden.append(act)
        slopes.append(slope)
    feed = contract(hidden[0], down_pair[0]) + contract(hidden[1], down_pair[1]) + down_bias
    block_out = (after_attention + mlp_scale * feed).astype(low)

    upstream = cotangent.astype(jnp.float32)
    grad_mlp_scale = jnp.sum(upstream * feed, axis=0)
    grad_feed = (upstream * mlp_scale).astype(low)
    grad_down_bias = jnp.sum(grad_feed.astype(jnp.float32), axis=0)
    down_sum, _ = sum_everywhere(
        *[contract_first(act, grad_feed).astype(low) for act in hidden], 0, parity, None
    )
    grad_pre = [
        (contract_last(grad_feed, weight) * slope.astype(jnp.float32)).astype(low)
        for weight, slope in zip(down_pair, slopes)
    ]
    grad_up_bias = [jnp.sum(part.astype(jnp.float32), axis=0) for part in grad_pre]
    up_sum, down_sum = sum_everywhere(
        *[contract_first(second_norm, part).astype(low) for part in grad_pre], 1, parity, down_sum
    )
    grad_second = contract_last(grad_pre[0], up_pair[0]) + contract_last(grad_pre[1], up_pair[1])
    _, second_pull = jax.vjp(norm_rows, after_attention, second_gain, second_bias)
    grad_after, grad_second_gain, grad_second_bias = second_pull(grad_second)
    grad_after = grad_after + upstream
    grad_attention_scale = jnp.sum(grad_after * attention, axis=0)
    grad_attention = (grad_after * attention_scale).astype(low)
    grad_out_bias = jnp.sum(grad_attention.astype(jnp.float32), axis=0)
    out_sum, up_sum = sum_everywhere(
        *[contract_first(part, grad_attention).astype(low) for part in mixed], 0, parity, up_sum
    )
    grad_projected = []
    grad_qv = []
    qkv_grads = []
    for part, log_part, weight in zip(projected, logs, out_pair):
        grad_mixed = contract_last(grad_attention, weight).astype(low)
        parts = attend_grad(part, grad_mixed, log_part)
        grad_qv.append(
            jnp.stack([jnp.sum(parts[j].astype(jnp.float32), axis=0) for j in (0, 2)])
        )
        grad_projected.append(jnp.concatenate(parts, axis=1))
        qkv_grads.append(jnp.stack([contract_first(first_norm, each).astype(low) for each in parts]))
    qkv_sum, out_sum = sum_everywhere(*qkv_grads, 2, parity, out_sum)
    grad_first = contract_last(grad_projected[0], qkv_pair[0]) + contract_last(
        grad_projected[1], qkv_pair[1]
    )
    _, first_pull = jax.vjp(norm_rows, residual, first_gain, first_bias)
    grad_input, grad_first_gain, grad_first_bias = first_pull(grad_first)
    grad_input = grad_input + grad_after

    place = lax.axis_index("tensor")

    def whole(own, other):
        other = in_order(other)
        first = jnp.where(place == 0, own, other)
        second = jnp.where(place == 0, other, own)
        return jnp.concatenate([first, second], axis=-1)

    shared = lax.psum(
        jnp.concatenate(
            [
                grad_first_gain,
                grad_first_bias,
                grad_out_bias,
                grad_attention_scale,
                grad_second_gain,
                grad_second_bias,
                grad_down_bias,
                grad_mlp_scale,
                whole(*grad_qv).reshape(-1),
                whole(*grad_up_bias),
            ]
        ),
        ("dp", "tensor"),
    )
    vectors = [shared[j * width : (j + 1) * width] for j in range(8)]
    qv_total = shared[8 * width : 8 * width + 4 * columns].reshape(2, 2 * columns)
    up_total = shared[8 * width + 4 * columns :]
    return (
        block_out,
        grad_input,
        vectors[0],
        vectors[1],
        both_halves(qkv_sum, 2, parity).transpose(1, 0, 2),
        lax.dynamic_slice_in_dim(qv_total, place * columns, columns, 1),
        both_halves(out_sum, 0, parity),
        vectors[2],
        vectors[3],
        vectors[4],
        vectors[5],
        both_halves(up_sum, 1, parity),
        lax.dynamic_slice_in_dim(up_total, place * units, units, 0),
        both_halves(down_sum, 0, parity),
        vectors[6],
        vectors[7],
    )


def body(tokens, *others):
    fits = tokens.shape[0] % SEQ == 0 and others[2].shape[2] % (2 * PAIR) == 0
    if fits and lax.axis_size("tensor") == 2 and lax.axis_size("dp") % 2 == 0:
        return image_body(tokens, *others)
    return general_body(tokens, *others)


def solution(mesh):
    return jax.shard_map(
        body,
        mesh=mesh,
        in_specs=(
            P(("dp", "tensor"), None),
            P(),
            P(),
            P(None, None, "tensor"),
            P(None, "tensor"),
            P("tensor", None),
            P(),
            P(),
            P(),
            P(),
            P(None, "tensor"),
            P("tensor"),
            P("tensor", None),
            P(),
            P(),
            P(("dp", "tensor"), None),
        ),
        out_specs=(
            P(("dp", "tensor"), None),
            P(("dp", "tensor"), None),
            P(),
            P(),
            P(None, None, "tensor"),
            P(None, "tensor"),
            P("tensor", None),
            P(),
            P(),
            P(),
            P(),
            P(None, "tensor"),
            P("tensor"),
            P("tensor", None),
            P(),
            P(),
        ),
        check_vma=False,
    )
```

```python
import math

import jax
import jax.numpy as jnp
from jax import lax
from jax.experimental import pallas as pl
from jax.experimental.pallas import tpu as pltpu
from jax.sharding import PartitionSpec as P

HD = 64
SEQ = 1024


EPSILON = 1e-06


def norm_rows(values, gain, shift):
    center = values - jnp.mean(values, axis=-1, keepdims=True)
    spread = jnp.mean(center * center, axis=-1, keepdims=True)
    return center * lax.rsqrt(spread + EPSILON) * gain + shift


def exact_gelu(values):
    return jax.nn.gelu(values, approximate=False)


def attend_forward(query, keys, values):
    factor = query.shape[-1] ** (-0.5)
    scores = jnp.einsum("qhd,khd->hqk", query, keys, preferred_element_type=jnp.float32) * factor
    row_peak = jnp.max(scores, axis=-1, keepdims=True)
    powers = jnp.exp(scores - row_peak)
    totals = jnp.sum(powers, axis=-1, keepdims=True)
    probs = (powers / totals).astype(jnp.bfloat16)
    mixed = jnp.einsum("hqk,khd->qhd", probs, values, preferred_element_type=jnp.float32).astype(
        jnp.bfloat16
    )
    return (mixed, row_peak[..., 0] + jnp.log(totals[..., 0]))


def attend_backward(carry, piece, keys, values):
    query, grad_out, log_totals = piece
    factor = query.shape[-1] ** (-0.5)
    scores = jnp.einsum("qhd,khd->hqk", query, keys, preferred_element_type=jnp.float32) * factor
    probs = jnp.exp(scores - log_totals[..., None])
    low_probs = probs.astype(jnp.bfloat16)
    grad_values = carry[1] + jnp.einsum(
        "hqk,qhd->khd", low_probs, grad_out, preferred_element_type=jnp.float32
    )
    grad_probs = jnp.einsum("qhd,khd->hqk", grad_out, values, preferred_element_type=jnp.float32)
    delta = jnp.sum(grad_probs * probs, axis=-1, keepdims=True)
    grad_scores = (probs * (grad_probs - delta)).astype(jnp.bfloat16)
    grad_query = (
        jnp.einsum("hqk,khd->qhd", grad_scores, keys, preferred_element_type=jnp.float32) * factor
    ).astype(jnp.bfloat16)
    grad_keys = (
        carry[0]
        + jnp.einsum("hqk,qhd->khd", grad_scores, query, preferred_element_type=jnp.float32)
        * factor
    )
    return ((grad_keys, grad_values), grad_query)


def general_body(
    tokens,
    first_gain,
    first_bias,
    qkv_weight,
    qv_bias,
    out_weight,
    out_bias,
    attention_scale,
    second_gain,
    second_bias,
    up_weight,
    up_bias,
    down_weight,
    down_bias,
    mlp_scale,
    cotangent,
):
    local_rows, width = tokens.shape
    group_size = lax.axis_size("tensor")
    total_rows = local_rows * group_size
    columns = qkv_weight.shape[2]
    heads_here = columns // HD
    block = min(512, SEQ)
    block_count = SEQ // block
    images = total_rows // SEQ
    image_shape = (images, SEQ, heads_here, HD)
    qkv_flat = qkv_weight.reshape(width, 3 * columns)
    residual = tokens.astype(jnp.float32)
    first_norm = norm_rows(residual, first_gain, first_bias).astype(jnp.bfloat16)
    normed = lax.all_gather(first_norm, "tensor", axis=0, tiled=True)
    projected = jnp.dot(normed, qkv_flat, preferred_element_type=jnp.float32)
    query = (projected[:, :columns] + qv_bias[0]).astype(jnp.bfloat16)
    keys = projected[:, columns : 2 * columns].astype(jnp.bfloat16)
    values = (projected[:, 2 * columns :] + qv_bias[1]).astype(jnp.bfloat16)

    def forward_image(parts):
        image_query, image_keys, image_values = parts
        blocks = image_query.reshape(block_count, block, heads_here, HD)
        mixed_blocks, log_blocks = lax.map(
            lambda piece: attend_forward(piece, image_keys, image_values), blocks
        )
        return (mixed_blocks.reshape(SEQ, heads_here, HD), log_blocks)

    mixed, log_totals = lax.map(
        forward_image,
        (query.reshape(image_shape), keys.reshape(image_shape), values.reshape(image_shape)),
    )
    mixed = mixed.reshape(total_rows, columns)
    attention = (
        lax.psum_scatter(
            jnp.dot(mixed, out_weight, preferred_element_type=jnp.float32),
            "tensor",
            scatter_dimension=0,
            tiled=True,
        )
        + out_bias
    )
    after_attention = residual + attention_scale * attention
    second_norm = norm_rows(after_attention, second_gain, second_bias).astype(jnp.bfloat16)
    normed_second = lax.all_gather(second_norm, "tensor", axis=0, tiled=True)
    pre_act = jnp.dot(normed_second, up_weight, preferred_element_type=jnp.float32) + up_bias
    activated, gelu_pull = jax.vjp(exact_gelu, pre_act)
    hidden = activated.astype(jnp.bfloat16)
    feed = (
        lax.psum_scatter(
            jnp.dot(hidden, down_weight, preferred_element_type=jnp.float32).astype(jnp.bfloat16),
            "tensor",
            scatter_dimension=0,
            tiled=True,
        ).astype(jnp.float32)
        + down_bias
    )
    block_out = (after_attention + mlp_scale * feed).astype(jnp.bfloat16)
    upstream = cotangent.astype(jnp.float32)
    grad_mlp_scale = jnp.sum(upstream * feed, axis=0)
    grad_feed = (upstream * mlp_scale).astype(jnp.bfloat16)
    grad_down_bias = jnp.sum(grad_feed.astype(jnp.float32), axis=0)
    feed_rows = lax.all_gather(grad_feed, "tensor", axis=0, tiled=True)
    grad_down_weight = jnp.dot(hidden.T, feed_rows, preferred_element_type=jnp.float32)
    grad_hidden = jnp.dot(feed_rows, down_weight.T, preferred_element_type=jnp.float32)
    grad_pre = gelu_pull(grad_hidden)[0].astype(jnp.bfloat16)
    grad_up_bias = jnp.sum(grad_pre.astype(jnp.float32), axis=0)
    grad_up_weight = jnp.dot(normed_second.T, grad_pre, preferred_element_type=jnp.float32)
    grad_second = lax.psum_scatter(
        jnp.dot(grad_pre, up_weight.T, preferred_element_type=jnp.float32),
        "tensor",
        scatter_dimension=0,
        tiled=True,
    )
    second_value, second_pull = jax.vjp(norm_rows, after_attention, second_gain, second_bias)
    grad_after, grad_second_gain, grad_second_bias = second_pull(grad_second)
    grad_after = grad_after + upstream
    grad_attention_scale = jnp.sum(grad_after * attention, axis=0)
    grad_attention = (grad_after * attention_scale).astype(jnp.bfloat16)
    grad_out_bias = jnp.sum(grad_attention.astype(jnp.float32), axis=0)
    attention_rows = lax.all_gather(grad_attention, "tensor", axis=0, tiled=True)
    grad_out_weight = jnp.dot(mixed.T, attention_rows, preferred_element_type=jnp.float32)
    grad_mixed = jnp.dot(attention_rows, out_weight.T, preferred_element_type=jnp.float32).astype(
        jnp.bfloat16
    )

    def backward_image(parts):
        image_query, image_keys, image_values, image_grad, image_logs = parts
        blocks = (
            image_query.reshape(block_count, block, heads_here, HD),
            image_grad.reshape(block_count, block, heads_here, HD),
            image_logs,
        )
        zeros = jnp.zeros((SEQ, heads_here, HD), jnp.float32)
        sums, grad_query_blocks = lax.scan(
            lambda carry, piece: attend_backward(carry, piece, image_keys, image_values),
            (zeros, zeros),
            blocks,
        )
        return (
            grad_query_blocks.reshape(SEQ, heads_here, HD),
            sums[0].astype(jnp.bfloat16),
            sums[1].astype(jnp.bfloat16),
        )

    grad_query, grad_keys, grad_values = lax.map(
        backward_image,
        (
            query.reshape(image_shape),
            keys.reshape(image_shape),
            values.reshape(image_shape),
            grad_mixed.reshape(image_shape),
            log_totals,
        ),
    )
    grad_query = grad_query.reshape(total_rows, columns)
    grad_keys = grad_keys.reshape(total_rows, columns)
    grad_values = grad_values.reshape(total_rows, columns)
    grad_qv_bias = jnp.stack(
        [
            jnp.sum(grad_query.astype(jnp.float32), axis=0),
            jnp.sum(grad_values.astype(jnp.float32), axis=0),
        ]
    )
    grad_projected = jnp.concatenate([grad_query, grad_keys, grad_values], axis=1)
    grad_qkv_weight = jnp.dot(normed.T, grad_projected, preferred_element_type=jnp.float32).reshape(
        width, 3, columns
    )
    grad_first = lax.psum_scatter(
        jnp.dot(grad_projected, qkv_flat.T, preferred_element_type=jnp.float32).astype(
            jnp.bfloat16
        ),
        "tensor",
        scatter_dimension=0,
        tiled=True,
    ).astype(jnp.float32)
    first_value, first_pull = jax.vjp(norm_rows, residual, first_gain, first_bias)
    grad_input, grad_first_gain, grad_first_bias = first_pull(grad_first)
    grad_input = grad_input + grad_after
    weights = (
        lax.psum(grad_qkv_weight.astype(jnp.bfloat16), "dp").astype(jnp.float32),
        lax.psum(grad_qv_bias.astype(jnp.bfloat16), "dp").astype(jnp.float32),
        lax.psum(grad_out_weight.astype(jnp.bfloat16), "dp").astype(jnp.float32),
        lax.psum(grad_up_weight.astype(jnp.bfloat16), "dp").astype(jnp.float32),
        lax.psum(grad_up_bias.astype(jnp.bfloat16), "dp").astype(jnp.float32),
        lax.psum(grad_down_weight.astype(jnp.bfloat16), "dp").astype(jnp.float32),
    )
    shared = lax.psum(
        (
            grad_first_gain,
            grad_first_bias,
            grad_out_bias,
            grad_attention_scale,
            grad_second_gain,
            grad_second_bias,
            grad_down_bias,
            grad_mlp_scale,
        ),
        ("dp", "tensor"),
    )
    return (
        block_out,
        grad_input,
        shared[0],
        shared[1],
        weights[0],
        weights[1],
        weights[2],
        shared[2],
        shared[3],
        shared[4],
        shared[5],
        weights[3],
        weights[4],
        weights[5],
        shared[6],
        shared[7],
    )


CHUNK = 256
PAIR = 2 * HD


def contract(left, right):
    return jnp.dot(left, right, preferred_element_type=jnp.float32)


def contract_last(left, right):
    return lax.dot_general(left, right, (((1,), (1,)), ((), ())), preferred_element_type=jnp.float32)


def contract_first(left, right):
    return lax.dot_general(left, right, (((0,), (0,)), ((), ())), preferred_element_type=jnp.float32)


def turned(values):
    return values.astype(jnp.float32).T.astype(jnp.bfloat16)


def pair_forward(query_ref, keys_ref, values_ref, mixed_ref, logs_ref):
    keys = keys_ref[...]
    query_t = turned(query_ref[...] * jnp.bfloat16(HD**-0.5))
    values_t = turned(values_ref[...])
    row_head = lax.broadcasted_iota(jnp.int32, (PAIR, SEQ), 0) // HD
    for head in range(2):
        own_query = jnp.where(row_head == head, query_t, jnp.zeros_like(query_t))
        own_values = values_t[head * HD : (head + 1) * HD]
        parts = []
        for start in range(0, SEQ, CHUNK):
            scores = contract(keys, own_query[:, start : start + CHUNK])
            peak = jnp.max(scores, axis=0, keepdims=True)
            powers = jnp.exp(scores - peak)
            totals = jnp.sum(powers, axis=0, keepdims=True)
            parts.append(contract(own_values, powers.astype(jnp.bfloat16)) / totals)
            logs_ref[0, head : head + 1, start : start + CHUNK] = peak + jnp.log(totals)
        mixed_ref[:, head * HD : (head + 1) * HD] = jnp.concatenate(parts, axis=1).T.astype(jnp.bfloat16)


def pair_backward(
    query_ref, keys_ref, values_ref, grad_ref, logs_ref, *others
):
    dq_ref, dk_ref, dv_ref, dk_sum, dv_sum = others[-5:]
    keys = keys_ref[...]
    values = values_ref[...]
    grad = grad_ref[...]
    query = query_ref[...] * jnp.bfloat16(HD**-0.5)
    query_t = turned(query)
    grad_t = turned(grad)
    keys_t = turned(keys)
    row_head = lax.broadcasted_iota(jnp.int32, (PAIR, SEQ), 0) // HD
    lane_head = lax.broadcasted_iota(jnp.int32, (SEQ, PAIR), 1) // HD
    zero = jnp.zeros_like(query)
    zero_t = jnp.zeros_like(query_t)
    for head in range(2):
        own_query_t = jnp.where(row_head == head, query_t, zero_t)
        own_grad_t = jnp.where(row_head == head, grad_t, zero_t)
        own_query = jnp.where(lane_head == head, query, zero)
        own_grad = jnp.where(lane_head == head, grad, zero)
        own_keys_t = keys_t[head * HD : (head + 1) * HD]
        parts = []
        for start in range(0, SEQ, CHUNK):
            cut = slice(start, start + CHUNK)
            scores = contract(keys, own_query_t[:, cut])
            probs = jnp.exp(scores - logs_ref[0, head : head + 1, cut])
            grad_probs = contract(values, own_grad_t[:, cut])
            delta = jnp.sum(grad_probs * probs, axis=0, keepdims=True)
            grad_scores = (probs * (grad_probs - delta)).astype(jnp.bfloat16)
            dv_part = contract(probs.astype(jnp.bfloat16), own_grad[cut])
            dk_part = contract(grad_scores, own_query[cut])
            if head == 0 and start == 0:
                dv_sum[...] = dv_part
                dk_sum[...] = dk_part
            else:
                dv_sum[...] += dv_part
                dk_sum[...] += dk_part
            parts.append(contract(own_keys_t, grad_scores) * HD**-0.5)
        dq_ref[:, head * HD : (head + 1) * HD] = jnp.concatenate(parts, axis=1).T.astype(jnp.bfloat16)
    dk_ref[...] = dk_sum[...].astype(jnp.bfloat16)
    dv_ref[...] = dv_sum[...].astype(jnp.bfloat16)


def part_spec(offset):
    return pl.BlockSpec((SEQ, PAIR), lambda image, pair: (image, offset + pair))


def logs_spec(pairs):
    return pl.BlockSpec((1, 2, SEQ), lambda image, pair: (image * pairs + pair, 0, 0))


def attend(projected):
    rows, columns = projected.shape[0], projected.shape[1] // 3
    pairs, images = columns // PAIR, rows // SEQ
    area = images * columns // HD * SEQ * SEQ
    return pl.pallas_call(
        pair_forward,
        grid=(images, pairs),
        in_specs=[part_spec(0), part_spec(pairs), part_spec(2 * pairs)],
        out_specs=[part_spec(0), logs_spec(pairs)],
        out_shape=[
            jax.ShapeDtypeStruct((rows, columns), jnp.bfloat16),
            jax.ShapeDtypeStruct((images * pairs, 2, SEQ), jnp.float32),
        ],
        compiler_params=pltpu.CompilerParams(vmem_limit_bytes=48 * 2**20),
        cost_estimate=pl.CostEstimate(
            flops=16 * area * HD, bytes_accessed=8 * rows * columns, transcendentals=area
        ),
    )(projected, projected, projected)


def attend_grad(projected, grad_mixed, logs, earlier):
    rows, columns = grad_mixed.shape
    pairs, images = columns // PAIR, rows // SEQ
    area = images * columns // HD * SEQ * SEQ
    return pl.pallas_call(
        pair_backward,
        grid=(images, pairs),
        in_specs=[
            part_spec(0),
            part_spec(pairs),
            part_spec(2 * pairs),
            part_spec(0),
            logs_spec(pairs),
        ]
        + [pl.BlockSpec(memory_space=pl.ANY)] * len(earlier),
        out_specs=[part_spec(0)] * 3,
        out_shape=[jax.ShapeDtypeStruct((rows, columns), jnp.bfloat16)] * 3,
        scratch_shapes=[pltpu.VMEM((SEQ, PAIR), jnp.float32)] * 2,
        compiler_params=pltpu.CompilerParams(vmem_limit_bytes=48 * 2**20),
        cost_estimate=pl.CostEstimate(
            flops=40 * area * HD, bytes_accessed=14 * rows * columns, transcendentals=area
        ),
    )(projected, projected, projected, grad_mixed, logs, *earlier)


def over_group(values):
    return lax.ppermute(values, "tensor", [(0, 1), (1, 0)])


def over_pair(values):
    size = lax.axis_size("dp")
    return lax.ppermute(values, "dp", [(index, index ^ 1) for index in range(size)])


def fetch(weight, axis, parity, earlier):
    half = weight.shape[axis] // 2
    near = over_group(lax.dynamic_slice_in_dim(weight, parity * half, half, axis))
    near, _ = lax.optimization_barrier((near, earlier))
    return jnp.concatenate([near, over_pair(near)], axis=axis)


def sum_four(own, other, axis, parity):
    half = own.shape[axis] // 2
    keep = lax.dynamic_slice_in_dim(own, parity * half, half, axis)
    give = lax.dynamic_slice_in_dim(own, (1 - parity) * half, half, axis)
    other_keep = lax.slice_in_dim(other, 0, half, axis=axis)
    other_give = lax.slice_in_dim(other, half, 2 * half, axis=axis)
    other_sum = other_keep + over_pair(other_give)
    own_sum = keep + over_pair(give)
    return own_sum + over_group(other_sum)


def sum_parity(quarter, after):
    if after is not None:
        quarter, after = lax.optimization_barrier((quarter, after))
    size = lax.axis_size("dp")
    groups = [list(range(0, size, 2)), list(range(1, size, 2))]
    return lax.psum(quarter, "dp", axis_index_groups=groups), after


def both_halves(summed, axis, parity):
    partner = over_pair(summed)
    low = jnp.where(parity == 0, summed, partner)
    high = jnp.where(parity == 0, partner, summed)
    return jnp.concatenate([low, high], axis=axis).astype(jnp.float32)


def image_body(
    tokens,
    first_gain,
    first_bias,
    qkv_weight,
    qv_bias,
    out_weight,
    out_bias,
    attention_scale,
    second_gain,
    second_bias,
    up_weight,
    up_bias,
    down_weight,
    down_bias,
    mlp_scale,
    cotangent,
):
    width = tokens.shape[1]
    columns = qkv_weight.shape[2]
    units = up_weight.shape[1]
    parity = lax.axis_index("dp") % 2
    low = jnp.bfloat16

    def in_order(values):
        half = values.shape[-1] // 2
        turned_round = jnp.concatenate([values[..., half:], values[..., :half]], axis=-1)
        return jnp.where(parity == 0, values, turned_round)

    qkv_own = qkv_weight.reshape(width, 3 * columns)
    half = columns // 2
    sent = jnp.concatenate(
        [
            lax.dynamic_slice_in_dim(qkv_own, j * columns + parity * half, half, 1)
            for j in range(3)
        ],
        axis=1,
    )
    near = over_group(sent)
    far = over_pair(near)
    qkv_other = jnp.concatenate(
        [piece[:, j * half : (j + 1) * half] for j in range(3) for piece in (near, far)], axis=1
    )
    biases = over_group(jnp.concatenate([qv_bias.reshape(-1), up_bias]))
    qv_other = in_order(biases[: 2 * columns].reshape(2, columns))
    up_bias_other = in_order(biases[2 * columns :])
    qkv_pair = (qkv_own, qkv_other)
    qv_pair = (qv_bias, qv_other)
    up_bias_pair = (up_bias, up_bias_other)

    residual = tokens.astype(jnp.float32)
    first_norm = norm_rows(residual, first_gain, first_bias).astype(low)
    projected = []
    mixed = []
    logs = []
    for weight, bias in zip(qkv_pair, qv_pair):
        shift = jnp.concatenate([bias[0], jnp.zeros_like(bias[0]), bias[1]])
        projected.append((contract(first_norm, weight) + shift).astype(low))
        part, log_part = attend(projected[-1])
        mixed.append(part)
        logs.append(log_part)
    out_pair = (out_weight, fetch(out_weight, 0, parity, mixed[0]))
    up_pair = (up_weight, fetch(up_weight, 1, parity, mixed[1]))
    down_pair = (down_weight, fetch(down_weight, 0, parity, mixed[1]))
    attention = contract(mixed[0], out_pair[0]) + contract(mixed[1], out_pair[1]) + out_bias
    after_attention = residual + attention_scale * attention
    second_norm = norm_rows(after_attention, second_gain, second_bias).astype(low)
    hidden = []
    slopes = []
    for weight, bias in zip(up_pair, up_bias_pair):
        pre_act = contract(second_norm, weight) + bias
        spread = 0.5 * (1.0 + lax.erf(pre_act * math.sqrt(0.5)))
        slope = spread + pre_act * jnp.exp(-0.5 * pre_act * pre_act) * (1.0 / math.sqrt(2.0 * math.pi))
        act, slope = lax.optimization_barrier(((pre_act * spread).astype(low), slope.astype(low)))
        hidden.append(act)
        slopes.append(slope)
    feed = contract(hidden[0], down_pair[0]) + contract(hidden[1], down_pair[1]) + down_bias
    block_out = (after_attention + mlp_scale * feed).astype(low)

    upstream = cotangent.astype(jnp.float32)
    grad_mlp_scale = jnp.sum(upstream * feed, axis=0)
    grad_feed = (upstream * mlp_scale).astype(low)
    grad_down_bias = jnp.sum(grad_feed.astype(jnp.float32), axis=0)
    down_quarter = sum_four(
        *[contract_first(act, grad_feed).astype(low) for act in hidden], 0, parity
    )
    down_sum, _ = sum_parity(down_quarter, None)
    grad_pre = [
        (contract_last(grad_feed, weight) * slope.astype(jnp.float32)).astype(low)
        for weight, slope in zip(down_pair, slopes)
    ]
    grad_up_bias = [jnp.sum(part.astype(jnp.float32), axis=0) for part in grad_pre]
    up_quarter = sum_four(
        *[contract_first(second_norm, part).astype(low) for part in grad_pre], 1, parity
    )
    up_sum, down_sum = sum_parity(up_quarter, down_sum)
    grad_second = contract_last(grad_pre[0], up_pair[0]) + contract_last(grad_pre[1], up_pair[1])
    _, second_pull = jax.vjp(norm_rows, after_attention, second_gain, second_bias)
    grad_after, grad_second_gain, grad_second_bias = second_pull(grad_second)
    grad_after = grad_after + upstream
    grad_attention_scale = jnp.sum(grad_after * attention, axis=0)
    grad_attention = (grad_after * attention_scale).astype(low)
    grad_out_bias = jnp.sum(grad_attention.astype(jnp.float32), axis=0)
    out_quarter = sum_four(
        *[contract_first(part, grad_attention).astype(low) for part in mixed], 0, parity
    )
    out_sum, up_sum = sum_parity(out_quarter, up_sum)
    earlier = ([down_quarter], [up_quarter, out_quarter, down_sum])
    grad_projected = []
    grad_qv = []
    qkv_grads = []
    for part, log_part, weight, ready in zip(projected, logs, out_pair, earlier):
        grad_mixed = contract_last(grad_attention, weight).astype(low)
        parts = attend_grad(part, grad_mixed, log_part, ready)
        grad_qv.append(
            jnp.stack([jnp.sum(parts[j].astype(jnp.float32), axis=0) for j in (0, 2)])
        )
        grad_projected.append(jnp.concatenate(parts, axis=1))
        qkv_grads.append(jnp.stack([contract_first(first_norm, each).astype(low) for each in parts]))
    qkv_sum, out_sum = sum_parity(sum_four(*qkv_grads, 2, parity), out_sum)
    grad_first = contract_last(grad_projected[0], qkv_pair[0]) + contract_last(
        grad_projected[1], qkv_pair[1]
    )
    _, first_pull = jax.vjp(norm_rows, residual, first_gain, first_bias)
    grad_input, grad_first_gain, grad_first_bias = first_pull(grad_first)
    grad_input = grad_input + grad_after

    place = lax.axis_index("tensor")

    def whole(own, other):
        other = in_order(other)
        first = jnp.where(place == 0, own, other)
        second = jnp.where(place == 0, other, own)
        return jnp.concatenate([first, second], axis=-1)

    shared = lax.psum(
        jnp.concatenate(
            [
                grad_first_gain,
                grad_first_bias,
                grad_out_bias,
                grad_attention_scale,
                grad_second_gain,
                grad_second_bias,
                grad_down_bias,
                grad_mlp_scale,
                whole(*grad_qv).reshape(-1),
                whole(*grad_up_bias),
            ]
        ),
        ("dp", "tensor"),
    )
    vectors = [shared[j * width : (j + 1) * width] for j in range(8)]
    qv_total = shared[8 * width : 8 * width + 4 * columns].reshape(2, 2 * columns)
    up_total = shared[8 * width + 4 * columns :]
    return (
        block_out,
        grad_input,
        vectors[0],
        vectors[1],
        both_halves(qkv_sum, 2, parity).transpose(1, 0, 2),
        lax.dynamic_slice_in_dim(qv_total, place * columns, columns, 1),
        both_halves(out_sum, 0, parity),
        vectors[2],
        vectors[3],
        vectors[4],
        vectors[5],
        both_halves(up_sum, 1, parity),
        lax.dynamic_slice_in_dim(up_total, place * units, units, 0),
        both_halves(down_sum, 0, parity),
        vectors[6],
        vectors[7],
    )


def body(tokens, *others):
    fits = tokens.shape[0] % SEQ == 0 and others[2].shape[2] % (2 * PAIR) == 0
    if fits and lax.axis_size("tensor") == 2 and lax.axis_size("dp") % 2 == 0:
        return image_body(tokens, *others)
    return general_body(tokens, *others)


def solution(mesh):
    return jax.shard_map(
        body,
        mesh=mesh,
        in_specs=(
            P(("dp", "tensor"), None),
            P(),
            P(),
            P(None, None, "tensor"),
            P(None, "tensor"),
            P("tensor", None),
            P(),
            P(),
            P(),
            P(),
            P(None, "tensor"),
            P("tensor"),
            P("tensor", None),
            P(),
            P(),
            P(("dp", "tensor"), None),
        ),
        out_specs=(
            P(("dp", "tensor"), None),
            P(("dp", "tensor"), None),
            P(),
            P(),
            P(None, None, "tensor"),
            P(None, "tensor"),
            P("tensor", None),
            P(),
            P(),
            P(),
            P(),
            P(None, "tensor"),
            P("tensor"),
            P("tensor", None),
            P(),
            P(),
        ),
        check_vma=False,
    )
```
